32 devices in a mesh: dp: 8 (over y, x, core), mp: 4 (over z).
Axes of the slice: x: 2, y: 2, z: 4, core: 2. Of those that a mesh axis runs over, the one named last changes fastest.
Arguments:
- hidden: bfloat16 [1024, 2560], P('dp', 'mp'), may hold values from -6 to 6
- norm_gain: bfloat16 [2560], replicated, may hold values from 0.5 to 1.5
- shared_gate: bfloat16 [2560, 3072], P(None, 'mp'), may hold values from -0.125 to 0.125
- shared_up: bfloat16 [2560, 3072], P(None, 'mp'), may hold values from -0.125 to 0.125
- shared_down: bfloat16 [3072, 2560], P('mp'), may hold values from -0.109375 to 0.109375
- expert_gate: bfloat16 [64, 2560, 1536], P('dp', None, 'mp'), may hold values from -0.125 to 0.125
- expert_up: bfloat16 [64, 2560, 1536], P('dp', None, 'mp'), may hold values from -0.125 to 0.125
- expert_down: bfloat16 [64, 1536, 2560], P('dp', 'mp'), may hold values from -0.15625 to 0.15625
- adapter_in: bfloat16 [64, 3072, 16], P('dp', 'mp'), may hold values from -0.109375 to 0.109375
- adapter_out: bfloat16 [64, 16, 2560], P('dp'), may hold values from -1.5 to 1.5
- active: int32 [16], replicated, may hold values from 0 to 63, as said below
- lengths: int32 [64], replicated, may hold values from 1 to 256, 1024 in all
- request_adapter: int32 [64], replicated, may hold values from 0 to 15
- routes: int32 [1024, 6], P('dp'), may hold values from 0 to 63, all different within a row; in each aligned block of 128 rows (0 to 127, 128 to 255, ...) at most 16 rows name the same one
- route_weights: float32 [1024, 6], P('dp'), may hold values from 0.05 to 0.35
Outputs:
- layer_out: bfloat16 [1024, 2560], P('dp', 'mp')
The draws below stay inside these ranges and needn't reach their ends.
Inputs may be any that keep to these rules, and one draw needn't show every extreme that they name: `active`: the entries are distinct. `routes`: within the 128 rows of one index of dp no expert is named more than 16 times, and that many is reached; a row names distinct experts.
All inputs are finite; a program needn't handle non-finite values.
Results may differ from the reference program's by a relative error of at most 0.015.
Values may be sent and summed in bfloat16 or wider, within the bound.
A program may use at most 128 MiB of HBM per device.

```python
import math
import jax
import jax.numpy as jnp
import numpy as np
from jax import lax

D = 2560
FF = 1536
SFF = 3072
EXPERTS = 64
TOPK = 6
ADAPTERS = 64
ACTIVE = 16
RANK = 16
TOK_DEV = 128
REQUESTS = 64
TOKENS = 1024
LONGEST = 256
CAP = 16
N_DP = 8


def draw_active(key, part):
    shuffled = jax.random.permutation(key, ADAPTERS)
    return shuffled[:ACTIVE].astype(jnp.int32)


def touch_ends(values, rng, low, largest):
    index_at = [jax.random.randint(jax.random.fold_in(rng, axis), (), 0, length) for axis, length in enumerate(values.shape)]
    main_axis = values.shape.index(max(values.shape))
    beside = index_at[:main_axis] + [(index_at[main_axis] + 1) % values.shape[main_axis]] + index_at[main_axis + 1:]
    return values.at[tuple(index_at)].set(low).at[tuple(beside)].set(largest)


def block_levels(own_key, shape, split, low, largest):
    gain, own = 1.0, jax.random.fold_in(own_key, 6)
    for position, blocks in split:
        heights = jnp.exp(jax.random.uniform(jax.random.fold_in(own, position), (blocks,), jnp.float32, low / len(split), largest / len(split)))
        gain = gain * jnp.repeat(heights, shape[position] // blocks).reshape([-1 if axis == position else 1 for axis in range(len(shape))])
    return gain


def profile(number_of, total, limit, skew):
    loads = [(1 << 20) // math.isqrt(rank ** skew) + 1 for rank in range(2, number_of + 1)]
    spare, counts = total - limit - (number_of - 1), [1] * (number_of - 1)
    while spare > 0:
        free = [i for i in range(number_of - 1) if counts[i] < limit]
        mass, budget = sum([loads[i] for i in free]), spare
        for i in free:
            more = min(limit - counts[i], max(1, budget * loads[i] // mass), spare)
            counts[i] = counts[i] + more
            spare = spare - more
    return np.array([limit] + counts)


def uneven_parts(key, amount, total, most, skew):
    if amount == 2:
        one = jax.random.randint(key, (), max(1, total - most), min(most, total - 1) + 1)
        return jnp.stack([one, total - one])
    tallies = jnp.asarray(profile(amount, total, most, skew), jnp.int32)
    twos = (amount - 1) // 2
    giver, taker = tallies[1:1 + 2 * twos:2], tallies[2:2 + 2 * twos:2]
    slack = jnp.minimum(giver - 1, most - taker)
    moved = jax.random.randint(jax.random.fold_in(key, 1), (twos,), 0, 1 << 20) % (slack + 1)
    tallies = tallies.at[1:1 + 2 * twos:2].set(giver - moved).at[2:2 + 2 * twos:2].set(taker + moved)
    return tallies[jax.random.permutation(jax.random.fold_in(key, 2), amount)]


def routed_block(own_key, own, number, rows, number_of, top, most, lean):
    ranking = jax.random.permutation(own_key, number_of)
    crowded, ordinary = load_shares(number_of, rows * top, most, lean, True), load_shares(number_of, rows * top, most, lean, False)
    places = jnp.arange(number_of)

    def named(sizes, turn):
        used = int((sizes > 0).sum())
        fixed = max(1, used // 4)
        moved = fixed + (places - fixed + turn * (used - fixed)) % max(1, number_of - fixed)
        return jnp.zeros((number_of,), jnp.int32).at[ranking[jnp.where(places < fixed, places, moved)]].set(jnp.asarray(sizes, jnp.int32))

    sizes = jnp.where(number % 4 == 0, named(crowded, number // 4), named(ordinary, number - number // 4 - 1))
    mixed = jax.random.permutation(jax.random.fold_in(own, 3), number_of)
    donor, taker = mixed[0:number_of // 2 * 2:2], mixed[1:number_of // 2 * 2:2]
    margin = jnp.minimum(sizes[donor] - 1, most - sizes[taker]) // 2
    margin = jnp.where((donor == ranking[0]) | (taker == ranking[0]) | (sizes[taker] == 0), 0, jnp.maximum(margin, 0))
    moved = jax.random.randint(jax.random.fold_in(own, 4), (number_of // 2,), 0, 1 << 20) % (margin + 1)
    sizes = sizes.at[donor].add(-moved).at[taker].add(moved)
    labels = jnp.searchsorted(jnp.cumsum(sizes), jnp.arange(rows * top), side="right").astype(jnp.int32)
    grid = labels.reshape(top, rows).T
    grid = grid[jax.random.permutation(jax.random.fold_in(own, 1), rows)]
    turn = jax.random.randint(jax.random.fold_in(own, 2), (rows, 1), 0, top)
    return jnp.take_along_axis(grid, (jnp.arange(top)[None, :] + turn) % top, axis=1)


def load_shares(count, total, limit, slope, full):
    portions = [(1 << 20) // math.isqrt(standing ** slope) + 1 for standing in range(1, count + 1)]
    largest = limit if full else min(limit, max(-(-total // count), total * portions[0] // sum(portions)))
    least = 1 if total - largest >= count - 1 else 0
    holding, surplus = [largest] + [least] * (count - 1), total - largest - least * (count - 1)
    while surplus > 0:
        movable = [i for i in range(1, count) if holding[i] < largest] or [i for i in range(1, count) if holding[i] < limit]
        pool, left = sum([portions[i] for i in movable]), surplus
        for i in movable:
            more = min(limit - holding[i], max(1, left * portions[i] // pool), surplus)
            holding[i] = holding[i] + more
            surplus = surplus - more
    return np.array(holding)


def scatter_about(rng, shape, scale, reach, pieces=(), kind=jnp.bfloat16):
    drawn = scale * jax.random.normal(rng, shape, jnp.float32)
    if pieces:
        drawn = drawn * block_levels(rng, shape, pieces, -0.22, 0.18)
    return jnp.clip(drawn, -reach, reach).astype(kind)


def setup_inputs(seed: int = 0) -> dict:
    key_list = jax.random.split(jax.random.key(seed), 16)
    hidden = scatter_about(key_list[0], (TOKENS, D), 1.0, 6.0, ((0, 8), (1, 4)))
    norm_gain = jnp.clip(1.0 + 0.1 * jax.random.normal(key_list[1], (D,), jnp.float32), 0.5, 1.5).astype(jnp.bfloat16)
    shared_gate = scatter_about(key_list[2], (D, SFF), D ** -0.5, 0.125, ((1, 4),))
    shared_up = scatter_about(key_list[3], (D, SFF), D ** -0.5, 0.125, ((1, 4),))
    shared_down = scatter_about(key_list[4], (SFF, D), SFF ** -0.5, 0.109375, ((0, 4),))
    expert_gate = scatter_about(key_list[5], (EXPERTS, D, FF), D ** -0.5, 0.125, ((0, 8), (2, 4)))
    expert_up = scatter_about(key_list[6], (EXPERTS, D, FF), D ** -0.5, 0.125, ((0, 8), (2, 4)))
    expert_down = scatter_about(key_list[7], (EXPERTS, FF, D), FF ** -0.5, 0.15625, ((0, 8), (1, 4)))
    adapter_in = scatter_about(key_list[8], (ADAPTERS, SFF, RANK), SFF ** -0.5, 0.109375, ((0, 8), (1, 4)))
    adapter_out = scatter_about(key_list[9], (ADAPTERS, RANK, D), RANK ** -0.5, 1.5, ((0, 8),))
    active = draw_active(jax.random.fold_in(key_list[15], 71), 0)
    lengths = uneven_parts(key_list[11], REQUESTS, TOKENS, LONGEST, 2).astype(jnp.int32)
    request_adapter = touch_ends(jax.random.randint(key_list[12], (REQUESTS,), 0, ACTIVE), jax.random.fold_in(key_list[12], 1), 0, ACTIVE - 1).astype(jnp.int32)
    routes_keys = jax.random.split(jax.random.fold_in(key_list[13], 1), TOKENS // TOK_DEV)
    routes_turns = jax.random.permutation(jax.random.fold_in(key_list[13], 3), TOKENS // TOK_DEV)
    routes = jax.vmap(lambda own, number: routed_block(jax.random.fold_in(key_list[13], 2), own, number, TOK_DEV, EXPERTS, TOPK, CAP, 1))(routes_keys, routes_turns).reshape((TOKENS, TOPK))
    route_weights = jnp.clip(0.05 + 0.29999999 * jax.random.uniform(key_list[14], (TOKENS, TOPK), jnp.float32) ** block_levels(key_list[14], (TOKENS, TOPK), ((0, 8),), -0.2, 0.2), 0.05, 0.35)
    return dict(hidden=hidden, norm_gain=norm_gain, shared_gate=shared_gate, shared_up=shared_up, shared_down=shared_down, expert_gate=expert_gate, expert_up=expert_up, expert_down=expert_down, adapter_in=adapter_in, adapter_out=adapter_out, active=active, lengths=lengths, request_adapter=request_adapter, routes=routes, route_weights=route_weights)


def rms_norm(hidden, norm_gain):
    values = hidden.astype(jnp.float32)
    factor = lax.rsqrt(lax.optimization_barrier(jnp.mean(values * values, axis=-1, keepdims=True)) + 1e-06)
    return (values * factor * norm_gain.astype(jnp.float32)).astype(jnp.bfloat16)

def reference(hidden, norm_gain, shared_gate, shared_up, shared_down, expert_gate, expert_up, expert_down, adapter_in, adapter_out, active, lengths, request_adapter, routes, route_weights):
    normed = rms_norm(hidden, norm_gain)
    shared_lin = jnp.dot(normed, shared_gate, preferred_element_type=jnp.float32)
    shared_pre = jnp.dot(normed, shared_up, preferred_element_type=jnp.float32)
    shared_act = (jax.nn.silu(shared_lin) * shared_pre).astype(jnp.bfloat16)
    request_end = jnp.cumsum(lengths).astype(jnp.int32)
    positions = jnp.arange(TOKENS, dtype=jnp.int32)
    request_of = lax.optimization_barrier(jnp.sum((request_end[None, :] <= positions[:, None]).astype(jnp.int32), axis=1))
    slot_of = request_adapter[request_of]
    chosen = (slot_of[:, None] == jnp.arange(ACTIVE, dtype=jnp.int32)[None, :]).astype(jnp.float32)
    in_matrix = jnp.transpose(adapter_in[active], (1, 0, 2)).reshape(SFF, ACTIVE * RANK)
    lowrank = jnp.dot(shared_act, in_matrix, preferred_element_type=jnp.float32)
    lowrank = (lowrank.reshape(TOKENS, ACTIVE, RANK) * chosen[:, :, None]).reshape(TOKENS, ACTIVE * RANK)
    out_matrix = adapter_out[active].reshape(ACTIVE * RANK, D).astype(jnp.float32)
    adapted = jnp.dot(lowrank, out_matrix, precision=lax.Precision.HIGHEST)
    shared_out = jnp.dot(shared_act, shared_down, preferred_element_type=jnp.float32) + adapted
    flat_routes = routes.reshape(-1)
    flat_weights = jnp.concatenate([route_weights.reshape(-1), jnp.zeros((1,), jnp.float32)])
    padded = jnp.concatenate([normed, jnp.zeros((1, D), normed.dtype)], axis=0)
    slot_count = N_DP * CAP

    def expert_step(total, layer):
        gate_weight, up_weight, down_weight, expert_id = layer
        hits = jnp.nonzero(flat_routes == expert_id, size=slot_count, fill_value=TOKENS * TOPK)[0].astype(jnp.int32)
        token_ids = hits // TOPK
        rows_in = padded[token_ids]
        gate_val = jnp.dot(rows_in, gate_weight, preferred_element_type=jnp.float32)
        up_val = jnp.dot(rows_in, up_weight, preferred_element_type=jnp.float32)
        inner = (jax.nn.silu(gate_val) * up_val).astype(jnp.bfloat16)
        result = jnp.dot(inner, down_weight, preferred_element_type=jnp.float32)
        total = total.at[token_ids].add(flat_weights[hits][:, None] * result)
        return (total, None)
    routed, _ = lax.scan(expert_step, jnp.zeros((TOKENS + 1, D), jnp.float32), (expert_gate, expert_up, expert_down, jnp.arange(EXPERTS, dtype=jnp.int32)))
    return (shared_out + routed[:TOKENS]).astype(jnp.bfloat16)
```

```python
import jax
import jax.numpy as jnp
from jax import lax
from jax.sharding import PartitionSpec as P

F32 = jnp.float32
BF16 = jnp.bfloat16


def body(
    hidden,
    norm_gain,
    shared_gate,
    shared_up,
    shared_down,
    expert_gate,
    expert_up,
    expert_down,
    adapter_in,
    adapter_out,
    active,
    lengths,
    request_adapter,
    routes,
    route_weights,
):
    rows, top = routes.shape
    dp = lax.axis_size("dp")
    mp = lax.axis_size("mp")
    me = lax.axis_index("dp")
    experts = expert_gate.shape[0]
    cap = mp * max(1, rows * top * 4 // (experts * dp * mp * 3))
    tokens = rows * dp
    table = jnp.concatenate([routes.astype(F32), route_weights], axis=1)
    table = lax.all_gather(table, "dp", axis=0, tiled=True)
    gathered = lax.all_gather(hidden, "mp", axis=1, tiled=True)
    values = gathered.astype(F32)
    factor = lax.rsqrt(jnp.mean(values * values, axis=-1, keepdims=True) + 1e-06)
    own_normed = (values * factor * norm_gain.astype(F32)).astype(BF16)
    normed = lax.all_gather(own_normed, "dp", axis=0, tiled=True)
    width = normed.shape[1]

    all_routes = table[:, :top].reshape(dp, rows, top)
    all_weights = table[:, top:].reshape(dp, rows, top)
    local = (me * experts + jnp.arange(experts, dtype=jnp.int32)).astype(F32)
    match = all_routes[..., None] == local
    hits = jnp.sum(match.astype(F32), axis=2)
    weight = jnp.sum(jnp.where(match, all_weights[..., None], 0.0), axis=2)
    lower = (jnp.arange(rows)[:, None] > jnp.arange(rows)[None, :]).astype(BF16)
    place = jnp.einsum("ut,stj->suj", lower, hits.astype(BF16), preferred_element_type=F32)
    place = jnp.where(hits > 0.5, place, -1.0)
    pick = place[..., None] == jnp.arange(cap, dtype=F32)
    slot_weight = jnp.sum(jnp.where(pick, weight[..., None], 0.0), axis=1)
    pick = pick.astype(BF16)

    slots_in = jnp.einsum("stjc,std->jscd", pick, normed.reshape(dp, rows, width), preferred_element_type=F32)
    slots_in = slots_in.astype(BF16).reshape(experts, dp * cap, width)
    gate_val = jnp.einsum("jcd,jdf->jcf", slots_in, expert_gate, preferred_element_type=F32)
    up_val = jnp.einsum("jcd,jdf->jcf", slots_in, expert_up, preferred_element_type=F32)
    inner = (jax.nn.silu(gate_val) * up_val).astype(BF16)
    result = jnp.einsum("jcf,jfd->jcd", inner, expert_down, preferred_element_type=F32)
    result = result.reshape(experts, dp, cap, width) * jnp.transpose(slot_weight, (1, 0, 2))[..., None]
    routed = jnp.einsum("stjc,jscd->std", pick, result.astype(BF16), preferred_element_type=F32)

    shared_lin = jnp.dot(normed, shared_gate, preferred_element_type=F32)
    shared_pre = jnp.dot(normed, shared_up, preferred_element_type=F32)
    shared_act = (jax.nn.silu(shared_lin) * shared_pre).astype(BF16)

    adapters, _, rank = adapter_in.shape
    request_end = jnp.cumsum(lengths)
    request_start = request_end - lengths
    positions = jnp.arange(tokens, dtype=jnp.int32)[:, None]
    inside = (positions >= request_start[None, :]) & (positions < request_end[None, :])
    pool_id = jnp.sum(
        jnp.where(request_adapter[:, None] == jnp.arange(active.shape[0])[None, :], active[None, :], 0), axis=1
    )
    adapter_of = jnp.sum(jnp.where(inside, pool_id[None, :], 0), axis=1)
    owned = me * adapters + jnp.arange(adapters * rank, dtype=jnp.int32) // rank
    chosen = adapter_of[:, None] == owned[None, :]
    in_matrix = jnp.transpose(adapter_in, (1, 0, 2)).reshape(shared_act.shape[1], adapters * rank)
    lowrank = jnp.dot(shared_act, in_matrix, preferred_element_type=F32)
    lowrank = jnp.where(chosen, lowrank, 0.0)
    high = lowrank.astype(BF16)
    adapted = jnp.dot(high, adapter_out.reshape(adapters * rank, width), preferred_element_type=F32)

    own_act = lax.dynamic_slice_in_dim(shared_act, me * rows, rows, axis=0)
    own_shared = jnp.dot(own_act, shared_down, preferred_element_type=F32)
    is_own = (jnp.arange(dp) == me)[:, None, None]
    total = routed + adapted.reshape(dp, rows, width) + jnp.where(is_own, own_shared[None], 0.0)
    total = total.astype(BF16).reshape(tokens, width)
    part = lax.psum_scatter(total, "dp", scatter_dimension=0, tiled=True)
    return lax.psum_scatter(part, "mp", scatter_dimension=1, tiled=True)


def solution(mesh):
    in_specs = (
        P("dp", "mp"),
        P(),
        P(None, "mp"),
        P(None, "mp"),
        P("mp", None),
        P("dp", None, "mp"),
        P("dp", None, "mp"),
        P("dp", "mp", None),
        P("dp", "mp", None),
        P("dp", None, None),
        P(),
        P(),
        P(),
        P("dp", None),
        P("dp", None),
    )
    return jax.shard_map(body, mesh=mesh, in_specs=in_specs, out_specs=P("dp", "mp"), check_vma=False)
```

```python
import functools

import jax
import jax.numpy as jnp
from jax import lax
from jax.experimental import pallas as pl
from jax.experimental.pallas import tpu as pltpu
from jax.sharding import PartitionSpec as P

F32 = jnp.float32
BF16 = jnp.bfloat16


MESH = pl.DeviceIdType.MESH


def other(me, bits):
    for bit in (1, 2, 4):
        if bits & bit:
            me = me + bit - 2 * bit * ((me // bit) % 2)
    return me


def greet(me, z, mp):
    barrier = pltpu.get_barrier_semaphore()
    for flip in (1, 2, 4):
        pl.semaphore_signal(barrier, inc=1, device_id={"dp": other(me, flip), "mp": z}, device_id_type=MESH)
    for k in range(1, mp):
        pl.semaphore_signal(barrier, inc=1, device_id={"dp": me, "mp": lax.rem(z + k, mp)}, device_id_type=MESH)
    pl.semaphore_wait(barrier, 3 + mp - 1)


def scatter_kernel(mp, total, out, near, first, second, final, parts, send_sem, recv_sem):
    me = lax.axis_index("dp")
    z = lax.axis_index("mp")
    width = total.shape[2]
    half = width // 2
    part = width // mp
    sides = (pl.ds(0, half), pl.ds(half, half))
    greet(me, z, mp)

    def send(src, dst, number, dp_to, mp_to):
        copy = pltpu.make_async_remote_copy(
            src_ref=src,
            dst_ref=dst,
            send_sem=send_sem.at[number],
            recv_sem=recv_sem.at[number],
            device_id={"dp": dp_to, "mp": mp_to},
            device_id_type=MESH,
        )
        copy.start()
        return copy

    order = (3, 1, 2, 0)
    near_copies = {r: send(total.at[other(me, 2 * r + 1)], near.at[r], r, other(me, 1), z) for r in order}
    flips = ((1, 2), (2, 1))
    first_copies = {}
    for r in order:
        near_copies[r].wait_recv()
        near[r] = (near[r].astype(F32) + total[other(me, 2 * r)].astype(F32)).astype(BF16)
        for side in range(2):
            one, two = flips[side]
            if r & one:
                late = 0 if r & two else 1
                first_copies[side, late] = send(
                    near.at[r, :, sides[side]], first.at[side, late], 4 + 2 * side + late, other(me, 2 * one), z
                )
    second_copies = []
    for side in range(2):
        one, two = flips[side]
        first_copies[side, 0].wait_recv()
        first[side, 0] = (first[side, 0].astype(F32) + near[two, :, sides[side]].astype(F32)).astype(BF16)
        second_copies.append(send(first.at[side, 0], second.at[side], 8 + side, other(me, 2 * two), z))
    for side in range(2):
        first_copies[side, 1].wait_recv()
        second_copies[side].wait_recv()
        whole = (
            near[0, :, sides[side]].astype(F32) + first[side, 1].astype(F32) + second[side].astype(F32)
        ).astype(BF16)
        for m in range(mp // 2):
            final[side * (mp // 2) + m] = whole[:, m * part : (m + 1) * part]
    part_copies = []
    for k in (2, 1, 3):
        to = lax.rem(z + k, mp)
        part_copies.append(send(final.at[to], parts.at[k - 1], 10 + k - 1, me, to))
    result = final[z].astype(F32)
    for copy, k in zip(part_copies, (2, 1, 3)):
        copy.wait_recv()
        result = result + parts[k - 1].astype(F32)
    out[...] = result.astype(BF16)
    for copy in [*near_copies.values(), *first_copies.values(), *second_copies, *part_copies]:
        copy.wait_send()


def reduce_scatter(total, mp):
    dp, rows, width = total.shape
    half = width // 2
    copies = 10 + mp - 1
    vmem = pl.BlockSpec(memory_space=pltpu.VMEM)
    return pl.pallas_call(
        functools.partial(scatter_kernel, mp),
        out_shape=jax.ShapeDtypeStruct((rows, width // mp), BF16),
        in_specs=[vmem],
        out_specs=vmem,
        scratch_shapes=[
            pltpu.VMEM((4, rows, width), BF16),
            pltpu.VMEM((2, 2, rows, half), BF16),
            pltpu.VMEM((2, rows, half), BF16),
            pltpu.VMEM((mp, rows, width // mp), BF16),
            pltpu.VMEM((mp - 1, rows, width // mp), BF16),
            pltpu.SemaphoreType.DMA((copies,)),
            pltpu.SemaphoreType.DMA((copies,)),
        ],
        compiler_params=pltpu.CompilerParams(collective_id=0, has_side_effects=True, vmem_limit_bytes=40 * 2**20),
    )(total)


def body(
    hidden,
    norm_gain,
    shared_gate,
    shared_up,
    shared_down,
    expert_gate,
    expert_up,
    expert_down,
    adapter_in,
    adapter_out,
    active,
    lengths,
    request_adapter,
    routes,
    route_weights,
):
    rows, top = routes.shape
    dp = lax.axis_size("dp")
    mp = lax.axis_size("mp")
    me = lax.axis_index("dp")
    experts = expert_gate.shape[0]
    cap = mp * max(1, rows * top * 4 // (experts * dp * mp * 3))
    tokens = rows * dp
    table = jnp.concatenate([routes.astype(F32), route_weights], axis=1)
    table = lax.all_gather(table, "dp", axis=0, tiled=True)
    gathered = lax.all_gather(hidden, "mp", axis=1, tiled=True)
    values = gathered.astype(F32)
    factor = lax.rsqrt(jnp.mean(values * values, axis=-1, keepdims=True) + 1e-06)
    own_normed = (values * factor * norm_gain.astype(F32)).astype(BF16)
    normed = lax.all_gather(own_normed, "dp", axis=0, tiled=True)
    width = normed.shape[1]

    all_routes = table[:, :top].reshape(dp, rows, top)
    all_weights = table[:, top:].reshape(dp, rows, top)
    local = (me * experts + jnp.arange(experts, dtype=jnp.int32)).astype(F32)
    match = all_routes[..., None] == local
    hits = jnp.sum(match.astype(F32), axis=2)
    weight = jnp.sum(jnp.where(match, all_weights[..., None], 0.0), axis=2)
    lower = (jnp.arange(rows)[:, None] > jnp.arange(rows)[None, :]).astype(BF16)
    place = jnp.einsum("ut,stj->suj", lower, hits.astype(BF16), preferred_element_type=F32)
    place = jnp.where(hits > 0.5, place, -1.0)
    pick = place[..., None] == jnp.arange(cap, dtype=F32)
    slot_weight = jnp.sum(jnp.where(pick, weight[..., None], 0.0), axis=1)
    pick = pick.astype(BF16)

    slots_in = jnp.einsum("stjc,std->jscd", pick, normed.reshape(dp, rows, width), preferred_element_type=F32)
    slots_in = slots_in.astype(BF16).reshape(experts, dp * cap, width)
    gate_val = jnp.einsum("jcd,jdf->jcf", slots_in, expert_gate, preferred_element_type=F32)
    up_val = jnp.einsum("jcd,jdf->jcf", slots_in, expert_up, preferred_element_type=F32)
    inner = (jax.nn.silu(gate_val) * up_val).astype(BF16)
    result = jnp.einsum("jcf,jfd->jcd", inner, expert_down, preferred_element_type=F32)
    result = result.reshape(experts, dp, cap, width) * jnp.transpose(slot_weight, (1, 0, 2))[..., None]
    routed = jnp.einsum("stjc,jscd->std", pick, result.astype(BF16), preferred_element_type=F32)

    shared_lin = jnp.dot(normed, shared_gate, preferred_element_type=F32)
    shared_pre = jnp.dot(normed, shared_up, preferred_element_type=F32)
    shared_act = (jax.nn.silu(shared_lin) * shared_pre).astype(BF16)

    adapters, _, rank = adapter_in.shape
    request_end = jnp.cumsum(lengths)
    request_start = request_end - lengths
    positions = jnp.arange(tokens, dtype=jnp.int32)[:, None]
    inside = (positions >= request_start[None, :]) & (positions < request_end[None, :])
    pool_id = jnp.sum(
        jnp.where(request_adapter[:, None] == jnp.arange(active.shape[0])[None, :], active[None, :], 0), axis=1
    )
    adapter_of = jnp.sum(jnp.where(inside, pool_id[None, :], 0), axis=1)
    owned = me * adapters + jnp.arange(adapters * rank, dtype=jnp.int32) // rank
    chosen = adapter_of[:, None] == owned[None, :]
    in_matrix = jnp.transpose(adapter_in, (1, 0, 2)).reshape(shared_act.shape[1], adapters * rank)
    lowrank = jnp.dot(shared_act, in_matrix, preferred_element_type=F32)
    lowrank = jnp.where(chosen, lowrank, 0.0)
    high = lowrank.astype(BF16)
    adapted = jnp.dot(high, adapter_out.reshape(adapters * rank, width), preferred_element_type=F32)

    own_act = lax.dynamic_slice_in_dim(shared_act, me * rows, rows, axis=0)
    own_shared = jnp.dot(own_act, shared_down, preferred_element_type=F32)
    is_own = (jnp.arange(dp) == me)[:, None, None]
    total = routed + adapted.reshape(dp, rows, width) + jnp.where(is_own, own_shared[None], 0.0)
    total = total.astype(BF16)
    if dp == 8 and mp == 4:
        return reduce_scatter(total, mp)
    total = total.reshape(tokens, width)
    part = lax.psum_scatter(total, "dp", scatter_dimension=0, tiled=True)
    return lax.psum_scatter(part, "mp", scatter_dimension=1, tiled=True)


def solution(mesh):
    in_specs = (
        P("dp", "mp"),
        P(),
        P(None, "mp"),
        P(None, "mp"),
        P("mp", None),
        P("dp", None, "mp"),
        P("dp", None, "mp"),
        P("dp", "mp", None),
        P("dp", "mp", None),
        P("dp", None, None),
        P(),
        P(),
        P(),
        P("dp", None),
        P("dp", None),
    )
    return jax.shard_map(body, mesh=mesh, in_specs=in_specs, out_specs=P("dp", "mp"), check_vma=False)
```

```python
import functools

import jax
import jax.numpy as jnp
from jax import lax
from jax.experimental import pallas as pl
from jax.experimental.pallas import tpu as pltpu
from jax.sharding import PartitionSpec as P

F32 = jnp.float32
BF16 = jnp.bfloat16


MESH = pl.DeviceIdType.MESH


def other(me, bits):
    for bit in (1, 2, 4):
        if bits & bit:
            me = me + bit - 2 * bit * ((me // bit) % 2)
    return me


def greet(me, z, mp):
    barrier = pltpu.get_barrier_semaphore()
    for flip in (1, 2, 4):
        pl.semaphore_signal(barrier, inc=1, device_id={"dp": other(me, flip), "mp": z}, device_id_type=MESH)
    for k in range(1, mp):
        pl.semaphore_signal(barrier, inc=1, device_id={"dp": me, "mp": lax.rem(z + k, mp)}, device_id_type=MESH)
    pl.semaphore_wait(barrier, 3 + mp - 1)


def scatter_kernel(mp, total, out, near, first, second, final, parts, send_sem, recv_sem):
    me = lax.axis_index("dp")
    z = lax.axis_index("mp")
    width = total.shape[2]
    half = width // 2
    part = width // mp
    sides = (pl.ds(0, half), pl.ds(half, half))
    greet(me, z, mp)

    def send(src, dst, number, dp_to, mp_to):
        copy = pltpu.make_async_remote_copy(
            src_ref=src,
            dst_ref=dst,
            send_sem=send_sem.at[number],
            recv_sem=recv_sem.at[number],
            device_id={"dp": dp_to, "mp": mp_to},
            device_id_type=MESH,
        )
        copy.start()
        return copy

    order = (3, 1, 2, 0)
    near_copies = {r: send(total.at[other(me, 2 * r + 1)], near.at[r], r, other(me, 1), z) for r in order}
    flips = ((1, 2), (2, 1))
    first_copies = {}
    for r in order:
        near_copies[r].wait_recv()
        near[r] = (near[r].astype(F32) + total[other(me, 2 * r)].astype(F32)).astype(BF16)
        for side in range(2):
            one, two = flips[side]
            if r & one:
                late = 0 if r & two else 1
                first_copies[side, late] = send(
                    near.at[r, :, sides[side]], first.at[side, late], 4 + 2 * side + late, other(me, 2 * one), z
                )
    second_copies = []
    for side in range(2):
        one, two = flips[side]
        first_copies[side, 0].wait_recv()
        first[side, 0] = (first[side, 0].astype(F32) + near[two, :, sides[side]].astype(F32)).astype(BF16)
        second_copies.append(send(first.at[side, 0], second.at[side], 8 + side, other(me, 2 * two), z))
    for side in range(2):
        first_copies[side, 1].wait_recv()
        second_copies[side].wait_recv()
        whole = (
            near[0, :, sides[side]].astype(F32) + first[side, 1].astype(F32) + second[side].astype(F32)
        ).astype(BF16)
        for m in range(mp // 2):
            final[side * (mp // 2) + m] = whole[:, m * part : (m + 1) * part]
    part_copies = []
    for k in (2, 1, 3):
        to = lax.rem(z + k, mp)
        part_copies.append(send(final.at[to], parts.at[k - 1], 10 + k - 1, me, to))
    result = final[z].astype(F32)
    for copy, k in zip(part_copies, (2, 1, 3)):
        copy.wait_recv()
        result = result + parts[k - 1].astype(F32)
    out[...] = result.astype(BF16)
    for copy in [*near_copies.values(), *first_copies.values(), *second_copies, *part_copies]:
        copy.wait_send()


def reduce_scatter(total, mp):
    dp, rows, width = total.shape
    half = width // 2
    copies = 10 + mp - 1
    vmem = pl.BlockSpec(memory_space=pltpu.VMEM)
    return pl.pallas_call(
        functools.partial(scatter_kernel, mp),
        out_shape=jax.ShapeDtypeStruct((rows, width // mp), BF16),
        in_specs=[vmem],
        out_specs=vmem,
        scratch_shapes=[
            pltpu.VMEM((4, rows, width), BF16),
            pltpu.VMEM((2, 2, rows, half), BF16),
            pltpu.VMEM((2, rows, half), BF16),
            pltpu.VMEM((mp, rows, width // mp), BF16),
            pltpu.VMEM((mp - 1, rows, width // mp), BF16),
            pltpu.SemaphoreType.DMA((copies,)),
            pltpu.SemaphoreType.DMA((copies,)),
        ],
        compiler_params=pltpu.CompilerParams(collective_id=0, has_side_effects=True, vmem_limit_bytes=40 * 2**20),
    )(total)


def body(
    hidden,
    norm_gain,
    shared_gate,
    shared_up,
    shared_down,
    expert_gate,
    expert_up,
    expert_down,
    adapter_in,
    adapter_out,
    active,
    lengths,
    request_adapter,
    routes,
    route_weights,
):
    rows, top = routes.shape
    dp = lax.axis_size("dp")
    mp = lax.axis_size("mp")
    me = lax.axis_index("dp")
    experts = expert_gate.shape[0]
    cap = mp * max(1, rows * top * 4 // (experts * dp * mp * 3))
    tokens = rows * dp
    table = jnp.concatenate([routes.astype(F32), route_weights], axis=1)
    table = lax.all_gather(table, "dp", axis=0, tiled=True)
    both = dp == 8 and mp == 4
    if both:
        gathered = lax.all_gather(hidden, ("dp", "mp"), axis=0, tiled=False)
        gathered = gathered.reshape(dp, mp, rows, hidden.shape[1])
        gathered = jnp.transpose(gathered, (0, 2, 1, 3)).reshape(tokens, mp * hidden.shape[1])
    else:
        gathered = lax.all_gather(hidden, "mp", axis=1, tiled=True)
    values = gathered.astype(F32)
    factor = lax.rsqrt(jnp.mean(values * values, axis=-1, keepdims=True) + 1e-06)
    normed = (values * factor * norm_gain.astype(F32)).astype(BF16)
    if not both:
        normed = lax.all_gather(normed, "dp", axis=0, tiled=True)
    width = normed.shape[1]

    all_routes = table[:, :top].reshape(dp, rows, top)
    all_weights = table[:, top:].reshape(dp, rows, top)
    local = (me * experts + jnp.arange(experts, dtype=jnp.int32)).astype(F32)
    match = all_routes[..., None] == local
    hits = jnp.sum(match.astype(F32), axis=2)
    weight = jnp.sum(jnp.where(match, all_weights[..., None], 0.0), axis=2)
    lower = (jnp.arange(rows)[:, None] > jnp.arange(rows)[None, :]).astype(BF16)
    place = jnp.einsum("ut,stj->suj", lower, hits.astype(BF16), preferred_element_type=F32)
    place = jnp.where(hits > 0.5, place, -1.0)
    pick = place[..., None] == jnp.arange(cap, dtype=F32)
    slot_weight = jnp.sum(jnp.where(pick, weight[..., None], 0.0), axis=1)
    pick = pick.astype(BF16)

    slots_in = jnp.einsum("stjc,std->jscd", pick, normed.reshape(dp, rows, width), preferred_element_type=F32)
    slots_in = slots_in.astype(BF16).reshape(experts, dp * cap, width)
    gate_val = jnp.einsum("jcd,jdf->jcf", slots_in, expert_gate, preferred_element_type=F32)
    up_val = jnp.einsum("jcd,jdf->jcf", slots_in, expert_up, preferred_element_type=F32)
    inner = (jax.nn.silu(gate_val) * up_val).astype(BF16)
    result = jnp.einsum("jcf,jfd->jcd", inner, expert_down, preferred_element_type=F32)
    result = result.reshape(experts, dp, cap, width) * jnp.transpose(slot_weight, (1, 0, 2))[..., None]
    routed = jnp.einsum("stjc,jscd->std", pick, result.astype(BF16), preferred_element_type=F32)

    shared_lin = jnp.dot(normed, shared_gate, preferred_element_type=F32)
    shared_pre = jnp.dot(normed, shared_up, preferred_element_type=F32)
    shared_act = (jax.nn.silu(shared_lin) * shared_pre).astype(BF16)

    adapters, _, rank = adapter_in.shape
    request_end = jnp.cumsum(lengths)
    request_start = request_end - lengths
    positions = jnp.arange(tokens, dtype=jnp.int32)[:, None]
    inside = (positions >= request_start[None, :]) & (positions < request_end[None, :])
    pool_id = jnp.sum(
        jnp.where(request_adapter[:, None] == jnp.arange(active.shape[0])[None, :], active[None, :], 0), axis=1
    )
    adapter_of = jnp.sum(jnp.where(inside, pool_id[None, :], 0), axis=1)
    owned = me * adapters + jnp.arange(adapters * rank, dtype=jnp.int32) // rank
    chosen = adapter_of[:, None] == owned[None, :]
    in_matrix = jnp.transpose(adapter_in, (1, 0, 2)).reshape(shared_act.shape[1], adapters * rank)
    lowrank = jnp.dot(shared_act, in_matrix, preferred_element_type=F32)
    lowrank = jnp.where(chosen, lowrank, 0.0)
    high = lowrank.astype(BF16)
    adapted = jnp.dot(high, adapter_out.reshape(adapters * rank, width), preferred_element_type=F32)

    own_act = lax.dynamic_slice_in_dim(shared_act, me * rows, rows, axis=0)
    own_shared = jnp.dot(own_act, shared_down, preferred_element_type=F32)
    is_own = (jnp.arange(dp) == me)[:, None, None]
    total = routed + adapted.reshape(dp, rows, width) + jnp.where(is_own, own_shared[None], 0.0)
    total = total.astype(BF16)
    if both:
        return reduce_scatter(total, mp)
    total = total.reshape(tokens, width)
    part = lax.psum_scatter(total, "dp", scatter_dimension=0, tiled=True)
    return lax.psum_scatter(part, "mp", scatter_dimension=1, tiled=True)


def solution(mesh):
    in_specs = (
        P("dp", "mp"),
        P(),
        P(None, "mp"),
        P(None, "mp"),
        P("mp", None),
        P("dp", None, "mp"),
        P("dp", None, "mp"),
        P("dp", "mp", None),
        P("dp", "mp", None),
        P("dp", None, None),
        P(),
        P(),
        P(),
        P("dp", None),
        P("dp", None),
    )
    return jax.shard_map(body, mesh=mesh, in_specs=in_specs, out_specs=P("dp", "mp"), check_vma=False)
```
